32 devices in a mesh: groups: 2 (over y), src: 16 (over z, x, core).
Axes of the slice: x: 2, y: 2, z: 4, core: 2. Of those that a mesh axis runs over, the one named last changes fastest.
Arguments:
- response: bfloat16 [256, 2, 2, 2, 1024, 512], P(('groups', 'src')), parts along dimension 0, may hold values from -0.09375 to 0.09375
- direct: bfloat16 [256, 2, 2, 32, 512], P(('groups', 'src')), parts along dimension 0, may hold values from -6 to 6
- arrival: int32 [4, 16384], P('groups', 'src'), parts along dimension 0, may hold values from 16 to 64
Outputs:
- minus: bfloat16 [256, 2, 2, 32, 512], P(('groups', 'src')), parts along dimension 0
- plus: bfloat16 [256, 2, 2, 32, 512], P(('groups', 'src')), parts along dimension 0
The draws below stay inside these ranges and needn't reach their ends.
There are 2 independent parts, one for each index of `groups`. The reference program is written for one: setup_inputs(seed, part) draws one part's arguments, and reference() takes and returns one part's arrays. A program takes and returns all parts, laid end to end along the dimension named above; each array names one. Nothing has to cross between parts.
All inputs are finite; a program needn't handle non-finite values.
Results may differ from the reference program's by a relative error of at most 0.011.
Values may be sent and summed in bfloat16 or wider, within the bound.
A program may use at most 384 MiB of HBM per device.

```python
import math
import jax
import jax.numpy as jnp
from jax import lax

NF = 64
NS = 1024
NP = 32
ITERS = 2
NT = 128


def set_ends(result, rng, least, top_value):
    shape = result.shape
    index_at = [jax.random.randint(jax.random.fold_in(rng, axis), (), 0, shape[axis]) for axis in range(len(shape))]
    result = result.at[tuple(index_at)].set(least)
    longest = shape.index(max(shape))
    index_at[longest] = (index_at[longest] + 1) % shape[longest]
    return result.at[tuple(index_at)].set(top_value)


def block_levels(own_key, extent, cuts, smallest, high):
    def one(axis_at, blocks):
        steps = jax.random.uniform(jax.random.fold_in(jax.random.fold_in(own_key, 6), axis_at), (blocks,), jnp.float32, smallest / len(cuts), high / len(cuts))
        return jnp.repeat(jnp.exp(steps), extent[axis_at] // blocks).reshape((-1,) + (1,) * (len(extent) - axis_at - 1))

    loudness = one(*cuts[0])
    for cut in cuts[1:]:
        loudness = loudness * one(*cut)
    return loudness


def gaussian(rng, dims, deviation, bound, pieces=(), kind=jnp.bfloat16):
    loudness = block_levels(rng, dims, pieces, -0.22, 0.18) if pieces else 1.0
    values = jax.random.normal(rng, dims, jnp.float32) * deviation * loudness
    return jnp.minimum(jnp.maximum(values, -bound), bound).astype(kind)


def setup_inputs(seed: int = 0, part: int = 0) -> dict:
    seeds = jax.random.split(jax.random.key(seed), 4)
    part_keys = jax.random.split(jax.random.fold_in(seeds[3], part), 4)
    response = gaussian(part_keys[0], (2 * NF, 2, 2, 2, NS, NS // 2), (4 * NS) ** -0.5, 0.09375, ((0, 16),))
    direct = gaussian(part_keys[1], (2 * NF, 2, 2, NP, NS // 2), 1.0, 6.0, ((0, 16),))
    arrival = set_ends(jax.random.randint(part_keys[2], (2, NS // 2 * NP), NT // 8, NT // 2 + 1), jax.random.fold_in(part_keys[2], 1), NT // 8, (NT // 2 + 1) - 1).astype(jnp.int32)
    return dict(response=response, direct=direct, arrival=arrival)


def transform_tables():
    sample_ids = jnp.arange(NT, dtype=jnp.int32)
    freq_ids = jnp.arange(NF, dtype=jnp.int32)
    phases = ((sample_ids[:, None] * freq_ids[None, :]) % NT).astype(jnp.float32) * (2.0 * math.pi / NT)
    weights = jnp.where(freq_ids == 0, 1.0, 2.0).astype(jnp.float32) / NT
    inverse = jnp.stack([weights[None, :] * jnp.cos(phases), -weights[None, :] * jnp.sin(phases)], axis=2)
    forward = jnp.stack([jnp.cos(phases).T, -jnp.sin(phases).T], axis=1)
    return inverse, forward


def apply_response(response, focusing, parity):
    def one_block(pair):
        block_resp, block_focus = pair
        split_resp = block_resp.reshape(2, 2, 2, 2, NS // 2, NS // 2).astype(jnp.float32)
        products = jnp.einsum('aijgsr,bjpr->abigps', split_resp, block_focus.astype(jnp.float32), precision=lax.Precision.HIGHEST)
        real_part = products[0, 0] - parity * products[1, 1]
        imag_part = products[0, 1] + parity * products[1, 0]
        return jnp.stack([real_part, imag_part], axis=0).astype(jnp.bfloat16)
    return lax.map(one_block, (response, focusing))


def windowed(partial_value, arrival, inverse, forward):
    summed = (partial_value[:NF].astype(jnp.float32) + partial_value[NF:].astype(jnp.float32)).astype(jnp.bfloat16)
    spectra = lax.optimization_barrier(summed).astype(jnp.float32)
    traces = jnp.einsum('tfq,fqigps->tigps', inverse, spectra, precision=lax.Precision.HIGHEST)
    sample_ids = jnp.arange(NT, dtype=jnp.int32)
    distance = jnp.minimum(sample_ids, NT - sample_ids)
    window_mask = (distance[:, None, None, None] < arrival.reshape(2, NP, NS // 2)[None]).astype(jnp.float32)
    traces = traces * window_mask[:, None]
    back = jnp.einsum('fqt,tigps->gfqips', forward, traces, precision=lax.Precision.HIGHEST).astype(jnp.bfloat16)
    return back.reshape(2 * NF, 2, 2, NP, NS // 2)


def reference(response, direct, arrival):
    inverse, forward = transform_tables()
    plus = direct
    minus = direct
    for iteration in range(ITERS):
        minus = windowed(apply_response(response, plus, 1.0), arrival, inverse, forward)
        update = windowed(apply_response(response, minus, -1.0), arrival, inverse, forward)
        plus = (direct.astype(jnp.float32) + update.astype(jnp.float32)).astype(jnp.bfloat16)
    return minus, plus
```

```python
import functools
import math

import jax
import jax.numpy as jnp
import numpy as np
from jax import lax
from jax.experimental import pallas as pl
from jax.experimental.pallas import tpu as pltpu
from jax.sharding import PartitionSpec as P

ITERS = 2
NT = 128
ROWS = 16
F32 = jnp.float32
BF16 = jnp.bfloat16


def transform_tables(nf):
    sample_ids = np.arange(NT)
    freq_ids = np.arange(nf)
    phases = (sample_ids[:, None] * freq_ids[None, :] % NT) * (2.0 * math.pi / NT)
    weights = np.where(freq_ids == 0, 1.0, 2.0) / NT
    inverse = np.stack([weights * np.cos(phases), -weights * np.sin(phases)], axis=2)
    forward = np.stack([np.cos(phases).T, -np.sin(phases).T], axis=1)
    return inverse.astype(np.float32), forward.astype(np.float32)


def split_table(table):
    high = table.astype(BF16)
    low = (table - high.astype(np.float32)).astype(BF16)
    return jnp.asarray(high), jnp.asarray(low)


def block_tables(nf, comps):
    inverse, forward = transform_tables(nf)
    eye = np.eye(comps, dtype=np.float32)
    inv = np.einsum("tfq,ij->itfqj", inverse, eye).reshape(comps * NT, nf * 2 * comps)
    fwd = np.einsum("fqt,ij->fqijt", forward, eye).reshape(nf * 2 * comps, comps * NT)
    return split_table(inv) + split_table(fwd)


def fill_left(x_ref, v, parity):
    points, width = v[0][0].shape
    for j in range(2):
        re, im = v[0][j], v[1][j]
        c0 = slice(j * width, (j + 1) * width)
        c1 = slice((2 + j) * width, (3 + j) * width)
        x_ref[:points, c0] = re
        x_ref[points:, c0] = im
        x_ref[:points, c1] = -im if parity > 0 else im
        x_ref[points:, c1] = re if parity > 0 else -re


def pass_kernel(parity, mode, *refs):
    r_ref, refs = refs[0], refs[1:]
    v_ref = d_ref = None
    if mode != "direct":
        v_ref, refs = refs[0], refs[1:]
    if mode != "plain":
        d_ref, refs = refs[0], refs[1:]
    arr_ref, ih_ref, il_ref, fh_ref, fl_ref, ret_ref = refs[:6]
    x_ref, part, arrived, spec, back, wout = refs[6:12]
    send_sem, recv_sem, rsend_sem, rrecv_sem, local_sem = refs[12:]
    devices, count, _, comps, _, lanes = part.shape
    points = x_ref.shape[0] // 2
    half = x_ref.shape[1] // 4
    sblocks = half // lanes
    pblocks = points // ROWS
    blocks = devices // 2
    k, i = pl.program_id(0), pl.program_id(1)
    me = lax.axis_index("src")
    barrier = pltpu.get_barrier_semaphore()

    @pl.when((k == 0) & (i == 0))
    def _():
        def greet(off, carry):
            to = lax.rem(me + off, devices)
            pl.semaphore_signal(
                barrier, inc=1, device_id={"src": to}, device_id_type=pl.DeviceIdType.MESH
            )
            return carry

        lax.fori_loop(1, devices, greet, 0)

    @pl.when(i == 0)
    def _():
        v = []
        for q in range(2):
            row = []
            for j in range(2):
                if mode == "direct":
                    row.append(d_ref[0, q, j])
                    continue
                val = jnp.concatenate(
                    [
                        jnp.concatenate(
                            [v_ref[a * sblocks + b, 0, q, j] for b in range(sblocks)], axis=1
                        )
                        for a in range(pblocks)
                    ],
                    axis=0,
                )
                if mode == "add":
                    val = (val.astype(F32) + d_ref[0, q, j].astype(F32)).astype(BF16)
                row.append(val)
            v.append(row)
        fill_left(x_ref, v, parity)

    wide = 256
    for g in range(2):
        for s0 in range(0, half, wide):
            acc = None
            for q in range(2):
                for j in range(2):
                    c = (q * 2 + j) * half
                    term = lax.dot_general(
                        x_ref[:, c : c + half],
                        r_ref[0, q, 0, j, g * half + s0 : g * half + s0 + wide, :],
                        (((1,), (1,)), ((), ())),
                        preferred_element_type=F32,
                    )
                    acc = term if acc is None else acc + term
            val = acc.astype(BF16)
            for q in range(2):
                for a in range(pblocks):
                    r0 = q * points + a * ROWS
                    for b in range(wide // lanes):
                        dest = (g * pblocks + a) * sblocks + s0 // lanes + b
                        part[dest, k, q, i] = val[r0 : r0 + ROWS, b * lanes : (b + 1) * lanes]

    @pl.when((k == 0) & (i == comps - 1))
    def _():
        pl.semaphore_wait(barrier, devices - 1)

    @pl.when(i == comps - 1)
    def _():
        def send(off, carry):
            to = lax.rem(me + off, devices)
            pltpu.make_async_remote_copy(
                src_ref=part.at[to, k],
                dst_ref=arrived.at[me, k],
                send_sem=send_sem,
                recv_sem=recv_sem,
                device_id={"src": to},
                device_id_type=pl.DeviceIdType.MESH,
            ).start()
            return carry

        lax.fori_loop(1, devices, send, 0)

    @pl.when((k == count - 1) & (i == comps - 1))
    def _():
        arrived[me] = part[me]
        every = pltpu.make_async_remote_copy(
            src_ref=part.at[pl.ds(0, devices - 1)],
            dst_ref=arrived.at[pl.ds(0, devices - 1)],
            send_sem=send_sem,
            recv_sem=recv_sem,
            device_id={"src": lax.rem(me + 1, devices)},
            device_id_type=pl.DeviceIdType.MESH,
        )
        every.wait_recv()
        chunk = 2 * comps * ROWS
        rows = blocks * count * chunk
        stride = rows // ROWS

        def add_up(n, carry):
            b, kk = n // count, lax.rem(n, count)
            total = arrived[b, kk].astype(F32) + arrived[blocks + b, kk].astype(F32)
            total = total.astype(BF16).astype(F32).reshape(chunk, lanes)
            spec[pl.ds(pl.multiple_of(n * chunk, chunk), chunk), :] = total
            return carry

        lax.fori_loop(0, blocks * count, add_up, 0)

        t = lax.rem(lax.broadcasted_iota(jnp.int32, (ih_ref.shape[0], lanes), 0), NT)
        dist = jnp.minimum(t, NT - t)
        for p in range(0, ROWS, 2):
            sp = jnp.concatenate(
                [spec[pl.ds(p + e, stride, stride=ROWS), :] for e in range(2)], axis=1
            ).astype(BF16)
            tr = jnp.dot(ih_ref[...], sp, preferred_element_type=F32) + jnp.dot(
                il_ref[...], sp, preferred_element_type=F32
            )
            mask = jnp.concatenate(
                [dist < arr_ref[p + e : p + e + 1, :] for e in range(2)], axis=1
            )
            tr = jnp.where(mask, tr, 0.0)
            high = tr.astype(BF16)
            low = (tr - high.astype(F32)).astype(BF16)
            res = (
                jnp.dot(fh_ref[...], high, preferred_element_type=F32)
                + jnp.dot(fh_ref[...], low, preferred_element_type=F32)
                + jnp.dot(fl_ref[...], high, preferred_element_type=F32)
            )
            for e in range(2):
                back[pl.ds(p + e, stride, stride=ROWS), :] = res[:, e * lanes : (e + 1) * lanes]

        def narrow(n, carry):
            b, kk = n // count, lax.rem(n, count)
            val = back[pl.ds(pl.multiple_of(n * chunk, chunk), chunk), :].astype(BF16)
            wout[b, kk] = val.reshape(2, comps, ROWS, lanes)
            return carry

        lax.fori_loop(0, blocks * count, narrow, 0)

        own = lax.rem(me, blocks)
        base = me - own
        keep = pltpu.make_async_copy(wout.at[own], ret_ref.at[own], local_sem)
        keep.start()

        def send_back(off, carry):
            to = lax.rem(own + off, blocks)
            pltpu.make_async_remote_copy(
                src_ref=wout.at[to],
                dst_ref=ret_ref.at[own],
                send_sem=rsend_sem,
                recv_sem=rrecv_sem,
                device_id={"src": base + to},
                device_id_type=pl.DeviceIdType.MESH,
            ).start()
            return carry

        lax.fori_loop(1, blocks, send_back, 0)
        every.wait_send()
        keep.wait()
        home = pltpu.make_async_remote_copy(
            src_ref=wout.at[pl.ds(0, blocks - 1)],
            dst_ref=ret_ref.at[pl.ds(0, blocks - 1)],
            send_sem=rsend_sem,
            recv_sem=rrecv_sem,
            device_id={"src": base + lax.rem(own + 1, blocks)},
            device_id_type=pl.DeviceIdType.MESH,
        )
        home.wait_recv()
        home.wait_send()


def round_trip(response, focusing, direct, arr, tables, parity, mode, lanes):
    count, _, comps, _, stations, half = response.shape
    points = direct.shape[3]
    blocks = (points // ROWS) * (half // lanes)
    rows = blocks * count * 2 * comps * ROWS
    d_spec = pl.BlockSpec((1, 2, 2, points, half), lambda k, i: (k, 0, 0, 0, 0))
    v_spec = pl.BlockSpec((blocks, 1, 2, 2, ROWS, lanes), lambda k, i: (0, k, 0, 0, 0, 0))
    operands = {"direct": (direct,), "plain": (focusing,), "add": (focusing, direct)}[mode]
    specs = {"direct": [d_spec], "plain": [v_spec], "add": [v_spec, d_spec]}[mode]
    whole = pl.BlockSpec(memory_space=pltpu.VMEM)
    return pl.pallas_call(
        functools.partial(pass_kernel, parity, mode),
        grid=(count, comps),
        in_specs=[pl.BlockSpec((1, 2, 1, 2, stations, half), lambda k, i: (k, 0, i, 0, 0, 0))]
        + specs
        + [whole] * 5,
        out_specs=pl.BlockSpec(memory_space=pl.ANY),
        out_shape=jax.ShapeDtypeStruct((blocks, count, 2, comps, ROWS, lanes), BF16),
        scratch_shapes=[
            pltpu.VMEM((2 * points, 4 * half), BF16),
            pltpu.VMEM((2 * blocks, count, 2, comps, ROWS, lanes), BF16),
            pltpu.VMEM((2 * blocks, count, 2, comps, ROWS, lanes), BF16),
            pltpu.VMEM((rows, lanes), F32),
            pltpu.VMEM((rows, lanes), F32),
            pltpu.VMEM((blocks, count, 2, comps, ROWS, lanes), BF16),
        ]
        + [pltpu.SemaphoreType.DMA] * 5,
        compiler_params=pltpu.CompilerParams(
            vmem_limit_bytes=48 * 2**20,
            collective_id={"direct": 0, "plain": 1, "add": 2}[mode],
            has_side_effects=True,
        ),
        name="round_trip",
    )(response, *operands, arr, *tables)


def fast_body(devices, lanes, response, direct, arrival):
    count, _, comps, _, _, half = response.shape
    points = direct.shape[3]
    sblocks = half // lanes
    blocks = devices // 2
    nf = count * blocks
    tables = block_tables(nf, comps)
    me = lax.axis_index("src")
    arr = lax.all_gather(arrival, "src", axis=1, tiled=True).reshape(2, points, half)
    own = lax.rem(me, blocks)
    arr = lax.dynamic_slice(
        arr,
        (me // blocks, own // sblocks * ROWS, lax.rem(own, sblocks) * lanes),
        (1, ROWS, lanes),
    )[0]

    def one_pass(focusing, parity, mode):
        return round_trip(response, focusing, direct, arr, tables, parity, mode, lanes)

    def natural(x):
        x = x.reshape(points // ROWS, sblocks, count, 2, comps, ROWS, lanes)
        return x.transpose(2, 3, 4, 0, 5, 1, 6).reshape(direct.shape)

    update = None
    for iteration in range(ITERS):
        minus = one_pass(update, 1.0, "add" if iteration else "direct")
        update = one_pass(minus, -1.0, "plain")
    plus = (direct.astype(F32) + natural(update).astype(F32)).astype(BF16)
    return natural(minus), plus


def plain_body(response, direct, arrival):
    count, _, comps, _, stations, half = response.shape
    points = direct.shape[3]
    nf = count * lax.axis_size("src") // 2
    inverse, forward = (jnp.asarray(x) for x in transform_tables(nf))
    sample_ids = jnp.arange(NT, dtype=jnp.int32)
    distance = jnp.minimum(sample_ids, NT - sample_ids)
    mask = (distance[:, None, None] < arrival[None]).astype(F32)

    def one_pass(focusing, parity):
        split = response.reshape(count, 2, comps, 2, 2, half, half)
        re, im = focusing[:, 0], focusing[:, 1]
        sign = jnp.asarray(parity, BF16)
        stacked = [jnp.stack([re, im], axis=1), jnp.stack([-sign * im, sign * re], axis=1)]
        total = None
        for part in range(2):
            for j in range(2):
                term = jnp.einsum(
                    "kigsr,kcpr->kcigps",
                    split[:, part, :, j],
                    stacked[part][:, :, j],
                    preferred_element_type=F32,
                )
                total = term if total is None else total + term
        shaped = total.astype(BF16).reshape(count, 2, comps, 2, points * half)
        arrived = lax.all_to_all(shaped, "src", split_axis=4, concat_axis=0, tiled=True)
        summed = (arrived[:nf].astype(F32) + arrived[nf:].astype(F32)).astype(BF16)
        spectra = lax.optimization_barrier(summed).astype(F32)
        highest = lax.Precision.HIGHEST
        traces = jnp.einsum("tfq,fqigb->tigb", inverse, spectra, precision=highest)
        traces = traces * mask[:, None]
        back = jnp.einsum("fqt,tigb->gfqib", forward, traces, precision=highest).astype(BF16)
        back = back.reshape(2 * nf, 2, comps, back.shape[-1])
        returned = lax.all_to_all(back, "src", split_axis=0, concat_axis=3, tiled=True)
        return returned.reshape(direct.shape)

    plus = minus = direct
    for _ in range(ITERS):
        minus = one_pass(plus, 1.0)
        update = one_pass(minus, -1.0)
        plus = (direct.astype(F32) + update.astype(F32)).astype(BF16)
    return minus, plus


def solution(mesh):
    devices = mesh.shape["src"]

    def body(response, direct, arrival):
        points, half = direct.shape[3:]
        lanes = points * half * 2 // (devices * ROWS)
        if points % ROWS or lanes % 128 or 256 % lanes:
            return plain_body(response, direct, arrival)
        return fast_body(devices, lanes, response, direct, arrival)

    in_specs = (
        P(("groups", "src"), None, None, None, None, None),
        P(("groups", "src"), None, None, None, None),
        P("groups", "src"),
    )
    out_specs = (
        P(("groups", "src"), None, None, None, None),
        P(("groups", "src"), None, None, None, None),
    )
    return jax.shard_map(body, mesh=mesh, in_specs=in_specs, out_specs=out_specs, check_vma=False)
```
